32 devices in a mesh: dp: 8 (over y, x, core), fsdp: 4 (over z).
Axes of the slice: x: 2, y: 2, z: 4, core: 2. Of those that a mesh axis runs over, the one named last changes fastest.
Arguments:
- tokens: bfloat16 [2, 2560, 1024], P(None, ('dp', 'fsdp')), may hold values from -6 to 6
- lengths: int32 [2, 8, 4], P(None, 'dp'), may hold values from 1 to 300, 320 in all within a row
- ln1_gain: bfloat16 [1024], P(('dp', 'fsdp')), may hold values from 0.5 to 1.5
- ln1_shift: bfloat16 [1024], P(('dp', 'fsdp')), may hold values from -1 to 1
- w_qkv: bfloat16 [1024, 3072], P(('dp', 'fsdp')), may hold values from -0.1875 to 0.1875
- q_bias: bfloat16 [1024], P(('dp', 'fsdp')), may hold values from -1 to 1
- v_bias: bfloat16 [1024], P(('dp', 'fsdp')), may hold values from -1 to 1
- w_out: bfloat16 [1024, 1024], P(('dp', 'fsdp')), may hold values from -0.75 to 0.75
- out_bias: bfloat16 [1024], P(('dp', 'fsdp')), may hold values from -1 to 1
- ln2_gain: bfloat16 [1024], P(('dp', 'fsdp')), may hold values from 0.5 to 1.5
- ln2_shift: bfloat16 [1024], P(('dp', 'fsdp')), may hold values from -1 to 1
- w_up: bfloat16 [1024, 4096], P(('dp', 'fsdp')), may hold values from -0.1875 to 0.1875
- up_bias: bfloat16 [4096], P(('dp', 'fsdp')), may hold values from -1 to 1
- w_down: bfloat16 [4096, 1024], P(('dp', 'fsdp')), may hold values from -0.09375 to 0.09375
- down_bias: bfloat16 [1024], P(('dp', 'fsdp')), may hold values from -1 to 1
- cotangent: bfloat16 [2, 2560, 1024], P(None, ('dp', 'fsdp')), may hold values from -6 to 6
Outputs:
- block_out: bfloat16 [2, 2560, 1024], P(None, ('dp', 'fsdp'))
- grad_tokens: bfloat16 [2, 2560, 1024], P(None, ('dp', 'fsdp'))
- grad_ln1_gain: float32 [1024], P(('dp', 'fsdp'))
- grad_ln1_shift: float32 [1024], P(('dp', 'fsdp'))
- grad_w_qkv: float32 [1024, 3072], P(('dp', 'fsdp'))
- grad_q_bias: float32 [1024], P(('dp', 'fsdp'))
- grad_v_bias: float32 [1024], P(('dp', 'fsdp'))
- grad_w_out: float32 [1024, 1024], P(('dp', 'fsdp'))
- grad_out_bias: float32 [1024], P(('dp', 'fsdp'))
- grad_ln2_gain: float32 [1024], P(('dp', 'fsdp'))
- grad_ln2_shift: float32 [1024], P(('dp', 'fsdp'))
- grad_w_up: float32 [1024, 4096], P(('dp', 'fsdp'))
- grad_up_bias: float32 [4096], P(('dp', 'fsdp'))
- grad_w_down: float32 [4096, 1024], P(('dp', 'fsdp'))
- grad_down_bias: float32 [1024], P(('dp', 'fsdp'))
The draws below stay inside these ranges and needn't reach their ends.
Inputs may be any that keep to these rules, and one draw needn't show every extreme that they name: Each row of 4 lengths sums to 320, and its longest is exactly a quarter of 80 short of 320.
All inputs are finite; a program needn't handle non-finite values.
Results may differ from the reference program's by a relative error of at most 0.012.
Values may be sent and summed in bfloat16 or wider, within the bound.
No kernel may reach another device: no remote copies, remote signals or barrier semaphores. Data moves between devices by JAX's collectives and lax.ppermute only.
A program may use at most 192 MiB of HBM per device.

```python
import math
import jax
import jax.numpy as jnp
import numpy as np
from jax import lax

D = 1024
H = 16
HD = 64
FF = 4096
TOK_DEV = 80
MB = 2
SEQS = 4
MB_TOK = 320
ROWS = 2560
N_DP = 8


def level_of(rng, dims, pieces, smallest, largest):
    loudness, own = 1.0, jax.random.fold_in(rng, 6)
    for dim, shards_of in pieces:
        heights = jnp.exp(jax.random.uniform(jax.random.fold_in(own, dim), (shards_of,), jnp.float32, smallest / len(pieces), largest / len(pieces)))
        loudness = loudness * jnp.repeat(heights, dims[dim] // shards_of).reshape([-1 if axis == dim else 1 for axis in range(len(dims))])
    return loudness


def profile(amount, total, limit, skew):
    portions = [(1 << 20) // math.isqrt(standing ** skew) + 1 for standing in range(2, amount + 1)]
    spare, holding = total - limit - (amount - 1), [1] * (amount - 1)
    while spare > 0:
        candidates = [i for i in range(amount - 1) if holding[i] < limit]
        pool, budget = sum([portions[i] for i in candidates]), spare
        for i in candidates:
            extra = min(limit - holding[i], max(1, budget * portions[i] // pool), spare)
            holding[i] = holding[i] + extra
            spare = spare - extra
    return np.array([limit] + holding)


def ragged(key, number_of, total, limit, skew):
    if number_of == 2:
        one = jax.random.randint(key, (), max(1, total - limit), min(limit, total - 1) + 1)
        return jnp.stack([one, total - one])
    tallies = jnp.asarray(profile(number_of, total, limit, skew), jnp.int32)
    couples = (number_of - 1) // 2
    donor, taker = tallies[1:1 + 2 * couples:2], tallies[2:2 + 2 * couples:2]
    room = jnp.minimum(donor - 1, limit - taker)
    passed = jax.random.randint(jax.random.fold_in(key, 1), (couples,), 0, 1 << 20) % (room + 1)
    tallies = tallies.at[1:1 + 2 * couples:2].set(donor - passed).at[2:2 + 2 * couples:2].set(taker + passed)
    return tallies[jax.random.permutation(jax.random.fold_in(key, 2), number_of)]


def normal_values(stream_key, extent, scale, most, cuts=(), kind=jnp.bfloat16):
    factor_of = level_of(stream_key, extent, cuts, -0.22, 0.18) if cuts else 1.0
    entries = jax.random.normal(stream_key, extent, jnp.float32) * scale * factor_of
    return jnp.minimum(jnp.maximum(entries, -most), most).astype(kind)


def setup_inputs(seed: int = 0) -> dict:
    keys = jax.random.split(jax.random.key(seed), 17)
    return {
        "tokens": normal_values(keys[0], (MB, ROWS, D), 1.0, 6.0, ((1, 32),)),
        "lengths": jax.vmap(lambda own: ragged(own, SEQS, MB_TOK, MB_TOK - TOK_DEV // 4, 2))(jax.random.split(keys[1], MB * N_DP)).reshape((MB, N_DP, SEQS)).astype(jnp.int32),
        "ln1_gain": jnp.clip(1.0 + 0.1 * jax.random.normal(keys[2], (D,), jnp.float32), 0.5, 1.5).astype(jnp.bfloat16),
        "ln1_shift": normal_values(keys[3], (D,), 0.2, 1.0, ((0, 32),)),
        "w_qkv": normal_values(keys[4], (D, 3 * D), D ** -0.5, 0.1875, ((0, 32),)),
        "q_bias": normal_values(keys[5], (D,), 0.2, 1.0, ((0, 32),)),
        "v_bias": normal_values(keys[6], (D,), 0.2, 1.0, ((0, 32),)),
        "w_out": normal_values(keys[7], (D, D), (D // 16) ** -0.5, 0.75, ((0, 32),)),
        "out_bias": normal_values(keys[8], (D,), 0.2, 1.0, ((0, 32),)),
        "ln2_gain": jnp.clip(1.0 + 0.1 * jax.random.normal(keys[9], (D,), jnp.float32), 0.5, 1.5).astype(jnp.bfloat16),
        "ln2_shift": normal_values(keys[10], (D,), 0.2, 1.0, ((0, 32),)),
        "w_up": normal_values(keys[11], (D, FF), D ** -0.5, 0.1875, ((0, 32),)),
        "up_bias": normal_values(keys[12], (FF,), 0.2, 1.0, ((0, 32),)),
        "w_down": normal_values(keys[13], (FF, D), FF ** -0.5, 0.09375, ((0, 32),)),
        "down_bias": normal_values(keys[14], (D,), 0.2, 1.0, ((0, 32),)),
        "cotangent": normal_values(keys[15], (MB, ROWS, D), 1.0, 6.0, ((1, 32),)),
    }


@jax.custom_vjp
def low(v):
    return lax.optimization_barrier(v.astype(jnp.bfloat16)).astype(jnp.float32)

@jax.custom_vjp
def low_back(v):
    return v

def low_keep(v):
    return (low(v), None)

def low_pass(kept, grad):
    return (grad,)

def back_keep(v):
    return (v, None)

def back_low(kept, grad):
    return (low(grad),)
low.defvjp(low_keep, low_pass)
low_back.defvjp(back_keep, back_low)

def rounded_both(value):
    return low(low_back(value))

def layer_norm(values, gain, shift):
    centre = lax.optimization_barrier(jnp.mean(values, axis=-1, keepdims=True))
    centred = values - centre
    spread = lax.optimization_barrier(jnp.mean(centred * centred, axis=-1, keepdims=True))
    return centred * lax.rsqrt(spread + 1e-05) * gain + shift

def product(left, right):
    return jnp.dot(left, right, precision=lax.Precision.HIGHEST)

def head_slopes():
    return jnp.exp2(-8.0 * (jnp.arange(H, dtype=jnp.float32) + 1.0) / H)

def block_forward(param_set, inputs, allowed, distance):
    gain_one, shift_one, full_qkv, bias_query, bias_value, full_out, bias_out, gain_two, shift_two, full_up, bias_up, full_down, bias_down = param_set
    normed = low(layer_norm(inputs, gain_one, shift_one))
    mixed = product(normed, full_qkv)
    query_rows = rounded_both(mixed[:, :D] + bias_query)
    key_rows = rounded_both(mixed[:, D:2 * D])
    value_rows = rounded_both(mixed[:, 2 * D:] + bias_value)
    count = inputs.shape[0]
    query_heads = query_rows.reshape(count, H, HD)
    key_heads = key_rows.reshape(count, H, HD)
    value_heads = value_rows.reshape(count, H, HD)
    raw_scores = jnp.einsum('qhd,khd->hqk', query_heads, key_heads, precision=lax.Precision.HIGHEST) * HD ** (-0.5)
    raw_scores = raw_scores - head_slopes()[:, None, None] * distance[None]
    raw_scores = low_back(raw_scores)
    raw_scores = jnp.where(allowed[None], raw_scores, -1e+30)
    row_top = lax.optimization_barrier(jnp.max(raw_scores, axis=-1, keepdims=True))
    exp_scores = jnp.exp(raw_scores - row_top)
    attn_probs = low(exp_scores / lax.optimization_barrier(jnp.sum(exp_scores, axis=-1, keepdims=True)))
    context = jnp.einsum('hqk,khd->qhd', attn_probs, value_heads, precision=lax.Precision.HIGHEST)
    context = rounded_both(context.reshape(count, D))
    attn_out = low_back(product(context, full_out) + bias_out)
    hidden = inputs + attn_out
    normed_mlp = low(layer_norm(hidden, gain_two, shift_two))
    up_proj = low_back(product(normed_mlp, full_up) + bias_up)
    activated = low(jax.nn.gelu(up_proj, approximate=True))
    down_proj = low_back(product(activated, full_down) + bias_down)
    return hidden + down_proj

def reference(tokens, lengths, ln1_gain, ln1_shift, w_qkv, q_bias, v_bias, w_out, out_bias, ln2_gain, ln2_shift, w_up, up_bias, w_down, down_bias, cotangent):
    param_set = tuple((weight_item.astype(jnp.float32) for weight_item in (ln1_gain, ln1_shift, w_qkv, q_bias, v_bias, w_out, out_bias, ln2_gain, ln2_shift, w_up, up_bias, w_down, down_bias)))
    positions = jnp.arange(MB_TOK, dtype=jnp.int32)
    distance = (positions[:, None] - positions[None, :]).astype(jnp.float32)
    inputs_all = tokens.astype(jnp.float32).reshape(MB * N_DP, MB_TOK, D)
    grads_all = cotangent.astype(jnp.float32).reshape(MB * N_DP, MB_TOK, D)
    seq_lengths = lengths.reshape(MB * N_DP, SEQS)
    grad_zero = tuple((jnp.zeros(weight_item.shape, jnp.float32) for weight_item in param_set))

    def step_batch(carry, batch_item):
        inputs_mb, lengths_mb, grad_mb = batch_item
        boundary = jnp.cumsum(lengths_mb)
        segment = lax.optimization_barrier(jnp.sum((positions[:, None] >= boundary[None, :]).astype(jnp.int32), axis=1))
        allowed = (segment[:, None] == segment[None, :]) & (positions[None, :] <= positions[:, None])
        output_mb, pull_back = jax.vjp(lambda params_in, rows_in: block_forward(params_in, rows_in, allowed, distance), param_set, inputs_mb)
        grad_params, grad_rows = pull_back(grad_mb)
        carry = jax.tree.map(lambda left, right: left + right, carry, grad_params)
        return (carry, (output_mb, grad_rows))
    grad_params, (outputs, grad_rows) = lax.scan(step_batch, grad_zero, (inputs_all, seq_lengths, grads_all))
    block_out = outputs.astype(jnp.bfloat16).reshape(MB, N_DP * MB_TOK, D)
    grad_tokens = grad_rows.astype(jnp.bfloat16).reshape(MB, N_DP * MB_TOK, D)
    return (block_out, grad_tokens, grad_params[0], grad_params[1], grad_params[2], grad_params[3], grad_params[4], grad_params[5], grad_params[6], grad_params[7], grad_params[8], grad_params[9], grad_params[10], grad_params[11], grad_params[12])
```

```python
import jax
import jax.numpy as jnp
from jax import lax
from jax.sharding import PartitionSpec as P

H = 16
HD = 64
F32 = jnp.float32
BF16 = jnp.bfloat16
BOTH = ("dp", "fsdp")


def mm(left, right):
    return jnp.dot(left, right, preferred_element_type=F32)


def mm_t(left, right):
    return lax.dot_general(left, right, (((1,), (1,)), ((), ())), preferred_element_type=F32)


def outer(lefts, rights):
    total = None
    for left, right in zip(lefts, rights):
        part = lax.dot_general(left, right, (((0,), (0,)), ((), ())), preferred_element_type=F32)
        total = part if total is None else total + part
    return total


def norm_parts(values):
    centred = values - jnp.mean(values, axis=-1, keepdims=True)
    scale = lax.rsqrt(jnp.mean(centred * centred, axis=-1, keepdims=True) + 1e-05)
    return centred * scale, scale


def norm_back(grad, unit, scale, gain):
    inner = grad * gain
    return scale * (
        inner
        - jnp.mean(inner, axis=-1, keepdims=True)
        - unit * jnp.mean(inner * unit, axis=-1, keepdims=True)
    )


def shift_perm(size, step):
    return [(i, (i + step) % size) for i in range(size)]


def xor_perm(size, bit):
    return [(i, i ^ bit) for i in range(size)]


def ring_gather(rows):
    size = lax.axis_size("fsdp")
    return jnp.concatenate(
        [rows] + [lax.ppermute(rows, "fsdp", shift_perm(size, s)) for s in range(1, size)], axis=0
    )


def ring_scatter(part):
    size = lax.axis_size("fsdp")
    step = part.shape[0] // size
    total = part[:step]
    for s in range(1, size):
        sent = part[s * step : (s + 1) * step].astype(BF16)
        total = total + lax.ppermute(sent, "fsdp", shift_perm(size, size - s)).astype(F32)
    return total


def bit_orders(size):
    bits = [1 << k for k in range(size.bit_length() - 1)]
    far, near = bits[1:], bits[:1]
    return [far + near, far[::-1] + near]


def cube_gather(rows, bits):
    size = lax.axis_size("dp")
    for bit in bits:
        rows = jnp.concatenate([rows, lax.ppermute(rows, "dp", xor_perm(size, bit))], axis=0)
    return rows


def cube_scatter(part, bits):
    size = lax.axis_size("dp")
    for bit in bits[::-1]:
        half = part.shape[0] // 2
        got = lax.ppermute(part[half:].astype(BF16), "dp", xor_perm(size, bit))
        part = part[:half] + got.astype(F32)
    return part


def dp_gather(block):
    size = lax.axis_size("dp")
    place = lax.axis_index("dp")
    block = block[None]
    bit = size // 2
    while bit:
        other = lax.ppermute(block, "dp", xor_perm(size, bit))
        high = (place & bit) != 0
        block = jnp.stack([jnp.where(high, other, block), jnp.where(high, block, other)], axis=1)
        block = block.reshape((-1,) + block.shape[2:])
        bit //= 2
    return block.reshape(-1, block.shape[-1])


def dp_scatter(part):
    size = lax.axis_size("dp")
    place = lax.axis_index("dp")
    part = part.reshape(size, -1, part.shape[-1])
    bit = 1
    while bit < size:
        pairs = part.reshape((-1, 2) + part.shape[1:])
        mine = jnp.where((place & bit) != 0, 1, 0)
        sent = lax.dynamic_index_in_dim(pairs, 1 - mine, axis=1, keepdims=False)
        kept = lax.dynamic_index_in_dim(pairs, mine, axis=1, keepdims=False)
        got = lax.ppermute(sent.astype(BF16), "dp", xor_perm(size, bit))
        part = kept.astype(F32) + got.astype(F32)
        bit *= 2
    return part.reshape(-1, part.shape[-1])


def heads_of(rows):
    return rows.reshape(rows.shape[0], -1, HD).transpose(1, 0, 2)


def rows_of(heads):
    return heads.transpose(1, 0, 2).reshape(heads.shape[1], -1)


def body(
    tokens,
    lengths,
    ln1_gain,
    ln1_shift,
    w_qkv,
    q_bias,
    v_bias,
    w_out,
    out_bias,
    ln2_gain,
    ln2_shift,
    w_up,
    up_bias,
    w_down,
    down_bias,
    cotangent,
):
    micro_count, tok_rows, width = tokens.shape
    dp_size, fs_size = lax.axis_size("dp"), lax.axis_size("fsdp")
    dp_at, fs_at = lax.axis_index("dp"), lax.axis_index("fsdp")
    own = w_qkv.shape[0]
    own_ff = w_down.shape[0]
    hidden_dev = w_up.shape[1] // dp_size
    head_cols = width // fs_size
    micros = range(micro_count)
    orders = bit_orders(dp_size)

    qkv_parts = w_qkv.reshape(own, 3, fs_size, head_cols).transpose(2, 0, 1, 3)
    qkv_parts = qkv_parts.reshape(fs_size, own, 3 * head_cols)
    qkv_rows = lax.all_to_all(qkv_parts, "fsdp", 0, 0).reshape(fs_size * own, 3 * head_cols)
    x_all = [ring_gather(tokens[m]) for m in micros]
    qkv_here = dp_gather(qkv_rows)
    vectors = [ln1_gain, ln1_shift, q_bias, v_bias, out_bias, ln2_gain, ln2_shift, down_bias, up_bias]
    small = jnp.concatenate(vectors)
    small = lax.all_to_all(
        jnp.broadcast_to(small, (dp_size * fs_size, small.shape[0])), BOTH, 0, 0, tiled=True
    )
    small = small.astype(F32)
    gain_one, shift_one, bias_query, bias_value, bias_out, gain_two, shift_two, bias_down = [
        small[:, k * own : (k + 1) * own].reshape(width) for k in range(8)
    ]
    bias_up = small[:, 8 * own :].reshape(-1)
    bias_query = lax.dynamic_slice_in_dim(bias_query, fs_at * head_cols, head_cols)
    bias_value = lax.dynamic_slice_in_dim(bias_value, fs_at * head_cols, head_cols)
    bias_up = lax.dynamic_slice_in_dim(bias_up, dp_at * hidden_dev, hidden_dev)
    swap = [(i, (i % dp_size) * fs_size + i // dp_size) for i in range(dp_size * fs_size)]
    out_here = lax.all_gather(lax.ppermute(w_out, BOTH, swap), "dp", axis=0, tiled=True)
    up_parts = w_up.reshape(own, dp_size, hidden_dev).transpose(1, 0, 2)
    up_rows = lax.all_to_all(up_parts, "dp", 0, 0)
    up_here = lax.all_gather(up_rows, "fsdp", axis=0)
    up_here = up_here.transpose(1, 0, 2, 3).reshape(width, hidden_dev)
    down_here = lax.all_gather(w_down, "fsdp", axis=0, tiled=True)
    g_all = [cube_gather(cotangent[m], orders[m % 2]) for m in micros]

    origin = (fs_at - jnp.arange(fs_size, dtype=jnp.int32)) % fs_size
    places = (origin[:, None] * tok_rows + jnp.arange(tok_rows, dtype=jnp.int32)[None]).reshape(-1)
    distance = (places[:, None] - places[None, :]).astype(F32)
    head_ids = fs_at * (H // fs_size) + jnp.arange(H // fs_size)
    slopes = jnp.exp2(-8.0 * (head_ids.astype(F32) + 1.0) / H)
    saved = []
    for m in micros:
        boundary = jnp.cumsum(lengths[m, 0])
        segment = jnp.sum((places[:, None] >= boundary[None, :]).astype(jnp.int32), axis=1)
        allowed = (segment[:, None] == segment[None, :]) & (places[None, :] <= places[:, None])
        unit, scale = norm_parts(x_all[m].astype(F32))
        normed = (unit * gain_one + shift_one).astype(BF16)
        mixed = mm(normed, qkv_here)
        query = heads_of((mixed[:, :head_cols] + bias_query).astype(BF16))
        key = heads_of(mixed[:, head_cols : 2 * head_cols].astype(BF16))
        value = heads_of((mixed[:, 2 * head_cols :] + bias_value).astype(BF16))
        scores = jnp.einsum("hqd,hkd->hqk", query, key, preferred_element_type=F32) * HD**-0.5
        scores = scores - slopes[:, None, None] * distance[None]
        scores = jnp.where(allowed[None], scores, -1e30)
        scores = jnp.exp(scores - jnp.max(scores, axis=-1, keepdims=True))
        probs = scores / jnp.sum(scores, axis=-1, keepdims=True)
        context = jnp.einsum("hqk,hkd->hqd", probs.astype(BF16), value, preferred_element_type=F32)
        context = rows_of(context.astype(BF16))
        attn = ring_scatter(mm(context, out_here))
        hidden = tokens[m].astype(F32) + attn + bias_out
        unit_two, scale_two = norm_parts(hidden)
        normed_two = cube_gather(
            (unit_two * gain_two + shift_two).astype(BF16), orders[m % 2]
        )
        saved.append(
            (normed, query, key, value, probs, context, hidden, unit_two, scale_two, normed_two)
        )

    outputs, d_attns, activated_all, d_up_all, sums = [], [], [], [], []
    for m in micros:
        hidden, unit_two, scale_two, normed_two = saved[m][6:]
        up_proj = mm(normed_two, up_here) + bias_up
        activated, gelu_pull = jax.vjp(lambda v: jax.nn.gelu(v, approximate=True), up_proj)
        d_up = gelu_pull(mm_t(g_all[m], down_here))[0].astype(BF16)
        d_normed_two = cube_scatter(mm_t(d_up, up_here), orders[m % 2])
        grad_out = cotangent[m].astype(F32)
        d_hidden = grad_out + norm_back(d_normed_two, unit_two, scale_two, gain_two)
        d_attn = d_hidden.astype(BF16)
        activated = activated.astype(BF16)
        block = cube_scatter(mm(activated, down_here), orders[m % 2])
        outputs.append((hidden + block + bias_down).astype(BF16))
        d_attns.append((d_hidden, d_attn))
        activated_all.append(activated)
        d_up_all.append(d_up)
        sums.append(
            (
                jnp.sum(d_normed_two * unit_two, axis=0),
                jnp.sum(d_normed_two, axis=0),
                jnp.sum(d_attn.astype(F32), axis=0),
                jnp.sum(grad_out, axis=0),
                jnp.sum(d_up.astype(F32), axis=0),
            )
        )
    grad_down = outer(activated_all, g_all).astype(BF16)
    grad_down = lax.psum_scatter(grad_down, "fsdp", scatter_dimension=0, tiled=True).astype(F32)
    grad_up = outer([part[9] for part in saved], d_up_all).astype(BF16)
    grad_up = grad_up.reshape(dp_size, fs_size, own, hidden_dev).transpose(1, 0, 2, 3)
    grad_up = lax.psum_scatter(grad_up, "fsdp", scatter_dimension=0, tiled=False)
    grad_up = lax.all_to_all(grad_up, "dp", 0, 0)
    grad_up = grad_up.transpose(1, 0, 2).reshape(own, -1).astype(F32)

    grad_rows, d_mixed_all, d_attn_all = [], [], []
    for m in micros:
        normed, query, key, value, probs, context = saved[m][:6]
        d_hidden, d_attn = d_attns[m]
        d_attn = ring_gather(d_attn)
        d_context = heads_of(mm_t(d_attn, out_here).astype(BF16))
        d_probs = jnp.einsum("hqd,hkd->hqk", d_context, value, preferred_element_type=F32)
        inner = jnp.sum(probs * d_probs, axis=-1, keepdims=True)
        d_score = (probs * (d_probs - inner)).astype(BF16)
        d_query = jnp.einsum("hqk,hkd->hqd", d_score, key, preferred_element_type=F32) * HD**-0.5
        d_key = jnp.einsum("hqk,hqd->hkd", d_score, query, preferred_element_type=F32) * HD**-0.5
        d_value = jnp.einsum(
            "hqk,hqd->hkd", probs.astype(BF16), d_context, preferred_element_type=F32
        )
        d_query, d_key, d_value = [rows_of(t.astype(BF16)) for t in (d_query, d_key, d_value)]
        d_mixed = jnp.concatenate([d_query, d_key, d_value], axis=1)
        d_normed = mm_t(d_mixed, qkv_here)
        unit, scale = norm_parts(x_all[m].astype(F32))
        sums[m] += (
            jnp.sum(d_normed * unit, axis=0),
            jnp.sum(d_normed, axis=0),
            jnp.sum(d_query.astype(F32), axis=0),
            jnp.sum(d_value.astype(F32), axis=0),
        )
        d_normed = ring_scatter(d_normed)
        d_input = norm_back(d_normed, unit[:tok_rows], scale[:tok_rows], gain_one)
        grad_rows.append((d_hidden + d_input).astype(BF16))
        d_mixed_all.append(d_mixed)
        d_attn_all.append(d_attn)
    grad_qkv = dp_scatter(outer([part[0] for part in saved], d_mixed_all).astype(BF16))
    grad_qkv = lax.all_to_all(
        grad_qkv.astype(BF16).reshape(fs_size, own, 3 * head_cols), "fsdp", 0, 0
    )
    grad_qkv = grad_qkv.reshape(fs_size, own, 3, head_cols).transpose(1, 2, 0, 3)
    grad_qkv = grad_qkv.reshape(own, 3 * width).astype(F32)
    grad_out = dp_scatter(outer([part[5] for part in saved], d_attn_all).astype(BF16))
    grad_out = lax.ppermute(grad_out, BOTH, [(b, a) for a, b in swap])

    sums = [sum(parts[1:], parts[0]) for parts in zip(*sums)]
    d_gain_two, d_shift_two, d_out_bias, d_down_bias, d_up_bias = sums[:5]
    d_gain_one, d_shift_one, d_q_bias, d_v_bias = sums[5:]

    def spread(part, total, at):
        return lax.dynamic_update_slice_in_dim(jnp.zeros((total,), F32), part, at, 0)

    d_q_bias = spread(d_q_bias, width, fs_at * head_cols)
    d_v_bias = spread(d_v_bias, width, fs_at * head_cols)
    d_up_bias = spread(d_up_bias, dp_size * hidden_dev, dp_at * hidden_dev)
    terms = [d_gain_one, d_shift_one, d_q_bias, d_v_bias]
    terms += [d_out_bias, d_gain_two, d_shift_two, d_down_bias, d_up_bias]
    terms = jnp.concatenate([t.reshape(dp_size * fs_size, -1) for t in terms], axis=1)
    terms = jnp.sum(lax.all_to_all(terms, BOTH, 0, 0, tiled=True), axis=0)
    d_gain_one, d_shift_one, d_q_bias, d_v_bias, d_out_bias, d_gain_two, d_shift_two, d_down_bias = [
        terms[k * own : (k + 1) * own] for k in range(8)
    ]
    d_up_bias = terms[8 * own :]
    return (
        jnp.stack(outputs, axis=0),
        jnp.stack(grad_rows, axis=0),
        d_gain_one,
        d_shift_one,
        grad_qkv,
        d_q_bias,
        d_v_bias,
        grad_out,
        d_out_bias,
        d_gain_two,
        d_shift_two,
        grad_up,
        d_up_bias,
        grad_down,
        d_down_bias,
    )


def solution(mesh):
    both = P(BOTH)
    rows = P(BOTH, None)
    toks = P(None, BOTH, None)
    return jax.shard_map(
        body,
        mesh=mesh,
        in_specs=(
            toks,
            P(None, "dp", None),
            both,
            both,
            rows,
            both,
            both,
            rows,
            both,
            both,
            both,
            rows,
            both,
            rows,
            both,
            toks,
        ),
        out_specs=(
            toks,
            toks,
            both,
            both,
            rows,
            both,
            both,
            rows,
            both,
            both,
            both,
            rows,
            both,
            rows,
            both,
        ),
        check_vma=False,
    )
```

```python
import functools

import jax
import jax.numpy as jnp
from jax import lax
from jax.experimental import pallas as pl
from jax.experimental.pallas import tpu as pltpu
from jax.sharding import PartitionSpec as P

H = 16
HD = 64
LANES = 128
F32 = jnp.float32
BF16 = jnp.bfloat16
BOTH = ("dp", "fsdp")


def mm(left, right):
    return jnp.dot(left, right, preferred_element_type=F32)


def mm_t(left, right):
    return lax.dot_general(left, right, (((1,), (1,)), ((), ())), preferred_element_type=F32)


def outer(lefts, rights):
    total = None
    for left, right in zip(lefts, rights):
        part = lax.dot_general(left, right, (((0,), (0,)), ((), ())), preferred_element_type=F32)
        total = part if total is None else total + part
    return total


def norm_parts(values):
    centred = values - jnp.mean(values, axis=-1, keepdims=True)
    scale = lax.rsqrt(jnp.mean(centred * centred, axis=-1, keepdims=True) + 1e-05)
    return centred * scale, scale


def norm_back(grad, unit, scale, gain):
    inner = grad * gain
    return scale * (
        inner
        - jnp.mean(inner, axis=-1, keepdims=True)
        - unit * jnp.mean(inner * unit, axis=-1, keepdims=True)
    )


def shift_perm(size, step):
    return [(i, (i + step) % size) for i in range(size)]


def xor_perm(size, bit):
    return [(i, i ^ bit) for i in range(size)]


def ring_gather(rows):
    size = lax.axis_size("fsdp")
    return [rows] + [lax.ppermute(rows, "fsdp", shift_perm(size, s)) for s in range(1, size)]


def ring_return(sent):
    size = lax.axis_size("fsdp")
    return [lax.ppermute(p, "fsdp", shift_perm(size, size - s)) for s, p in enumerate(sent, 1)]


def bit_orders(size):
    bits = [1 << k for k in range(size.bit_length() - 1)]
    far, near = bits[1:], bits[:1]
    return [far + near, far[::-1] + near]


def cube_gather(rows, bits):
    size = lax.axis_size("dp")
    for bit in bits[:-1]:
        rows = jnp.concatenate([rows, lax.ppermute(rows, "dp", xor_perm(size, bit))], axis=0)
    return rows, lax.ppermute(rows, "dp", xor_perm(size, bits[-1]))


def cube_scatter(kept, sent, bits):
    size = lax.axis_size("dp")
    for bit in bits[:0:-1]:
        kept, sent = add_split(kept, lax.ppermute(sent, "dp", xor_perm(size, bit)))
    return kept, lax.ppermute(sent, "dp", xor_perm(size, bits[0]))


def dp_gather(block, bits):
    size = lax.axis_size("dp")
    place = lax.axis_index("dp")
    done = []
    for bit in bits:
        other = lax.ppermute(block, "dp", xor_perm(size, bit))
        high = (place & bit) != 0
        axis = sum(b > bit for b in done)
        block = jnp.stack([jnp.where(high, other, block), jnp.where(high, block, other)], axis=axis)
        done.append(bit)
    return block.reshape(-1, block.shape[-1])


def dp_scatter(part, bits):
    size = lax.axis_size("dp")
    place = lax.axis_index("dp")
    left = sorted(bits, reverse=True)
    part = part.reshape((2,) * len(bits) + (part.shape[0] // size, part.shape[1]))
    for bit in bits[::-1]:
        axis = left.index(bit)
        left.remove(bit)
        mine = jnp.where((place & bit) != 0, 1, 0)
        sent = lax.dynamic_index_in_dim(part, 1 - mine, axis=axis, keepdims=False)
        kept = lax.dynamic_index_in_dim(part, mine, axis=axis, keepdims=False)
        got = lax.ppermute(sent.astype(BF16), "dp", xor_perm(size, bit))
        part = kept.astype(F32) + got.astype(F32)
    return part


def together(*values):
    return lax.optimization_barrier(values)


def pack(vectors, own):
    lead = vectors[0].shape[:-1]
    if own >= len(vectors):
        spare = [LANES - v.shape[-1] for v in vectors]
        rows = [jnp.pad(v, [(0, 0)] * len(lead) + [(0, n)]) for v, n in zip(vectors, spare)]
        block = jnp.stack(rows, axis=-2)
        return jnp.pad(block, [(0, 0)] * len(lead) + [(0, own - len(vectors)), (0, 0)])
    block = jnp.concatenate(vectors, axis=-1)
    block = jnp.pad(block, [(0, 0)] * len(lead) + [(0, own * LANES - block.shape[-1])])
    return block.reshape(lead + (own, LANES))


def unpack(block, own, own_ff):
    lead = block.shape[:-2]
    if own >= 9:
        return block[..., :8, :own], block[..., 8, :own_ff]
    block = block.reshape(lead + (-1,))
    return block[..., : 8 * own].reshape(lead + (8, own)), block[..., 8 * own : 8 * own + own_ff]


def run(kernel, outs, ins, flops, scratch=(), smem=0):
    here = pl.BlockSpec(memory_space=pltpu.VMEM)
    moved = sum(v.size * v.dtype.itemsize for v in list(outs) + list(ins))
    return pl.pallas_call(
        kernel,
        out_shape=outs,
        in_specs=[pl.BlockSpec(memory_space=pltpu.SMEM)] * smem + [here] * (len(ins) - smem),
        out_specs=[here] * len(outs),
        scratch_shapes=scratch,
        compiler_params=pltpu.CompilerParams(vmem_limit_bytes=moved + 12 * 1024 * 1024),
        cost_estimate=pl.CostEstimate(flops=int(flops), bytes_accessed=moved, transcendentals=0),
    )(*ins)


def shape(dims, dtype):
    return jax.ShapeDtypeStruct(dims, dtype)


def add_split_kernel(kept, got, new_kept, new_sent):
    half = new_kept.shape[0]
    new_kept[...] = kept[:half] + got[:half].astype(F32)
    new_sent[...] = (kept[half:] + got[half:].astype(F32)).astype(BF16)


def add_split(kept, got):
    half = (kept.shape[0] // 2, kept.shape[1])
    return run(add_split_kernel, [shape(half, F32), shape(half, BF16)], [kept, got], kept.size)


def split_kernel(fs_size, at, w_qkv, small, *outs):
    cols = w_qkv.shape[1] // (3 * fs_size)
    for s, out in enumerate(outs):
        to = lax.rem(at[0] + s, fs_size) * cols
        for k, put in ((0, 0), (1, cols), (2, 2 * cols + LANES)):
            start = pl.multiple_of(to + k * fs_size * cols, LANES)
            out[:, put : put + cols] = w_qkv[:, pl.ds(start, cols)]
        out[:, 2 * cols : 2 * cols + LANES] = small[...]


def join_kernel(fs_size, at, *refs):
    pieces, (out, small) = refs[:fs_size], refs[fs_size:]
    cols = out.shape[1] // (3 * fs_size)
    total = 0.0
    for s, piece in enumerate(pieces):
        to = lax.rem(at[0] + fs_size - s, fs_size) * cols
        for k, put in ((0, 0), (1, cols), (2, 2 * cols + LANES)):
            start = pl.multiple_of(to + k * fs_size * cols, LANES)
            out[:, pl.ds(start, cols)] = piece[:, put : put + cols].astype(F32)
        total = total + piece[:, 2 * cols : 2 * cols + LANES].astype(F32)
    small[...] = total


def positions(meta, index, step, fs_size):
    place = index + meta[0] * step
    for s in range(1, fs_size):
        turn = jnp.where(meta[0] - s == -1, fs_size - 2, -2)
        place = place + jnp.where(index >= s * step, turn * step, 0)
    seg = jnp.zeros_like(index)
    for k in range(1, meta.shape[0]):
        seg = seg + jnp.where(place >= meta[k], 1, 0)
    return place, seg


def attend_kernel(fs_size, meta, slopes, *refs):
    chunks, refs = refs[:fs_size], refs[fs_size:]
    small, biases, w_qk, w_v, w_out, kept, *sent = refs[: 5 + fs_size]
    normed, query, key, value, probs, context = refs[5 + fs_size :]
    step = kept.shape[0]
    rows, cols = query.shape
    for s, chunk in enumerate(chunks):
        unit, _ = norm_parts(chunk[...].astype(F32))
        normed[s * step : (s + 1) * step] = (unit * small[0:1] + small[1:2]).astype(BF16)
    query[...] = (mm(normed[...], w_qk[:, :cols]) + biases[0:1]).astype(BF16)
    key[...] = mm(normed[...], w_qk[:, cols:]).astype(BF16)
    value[...] = (mm(normed[...], w_v[...]) + biases[1:2]).astype(BF16)
    row_place, row_seg = positions(meta, lax.broadcasted_iota(jnp.int32, (rows, 1), 0), step, fs_size)
    col_place, col_seg = positions(meta, lax.broadcasted_iota(jnp.int32, (1, rows), 1), step, fs_size)
    allowed = (row_seg == col_seg) & (col_place <= row_place)
    distance = (row_place - col_place).astype(F32)
    for h in range(cols // HD):
        part = slice(h * HD, (h + 1) * HD)
        scores = mm_t(query[:, part], key[:, part]) * HD**-0.5 - slopes[h] * distance
        scores = jnp.where(allowed, scores, -1e30)
        scores = jnp.exp(scores - jnp.max(scores, axis=-1, keepdims=True))
        scores = scores / jnp.sum(scores, axis=-1, keepdims=True)
        probs[h] = scores
        context[:, part] = mm(scores.astype(BF16), value[:, part]).astype(BF16)
    kept[...] = mm(context[:step], w_out[...])
    for s, piece in enumerate(sent, 1):
        piece[...] = mm(context[s * step : (s + 1) * step], w_out[...]).astype(BF16)


def hidden_kernel(fs_size, x, kept, *refs):
    got, (small, hidden, normed) = refs[: fs_size - 1], refs[fs_size - 1 :]
    total = kept[...]
    for piece in got:
        total = total + piece[...].astype(F32)
    total = x[...].astype(F32) + total + small[4:5]
    hidden[...] = total
    unit, _ = norm_parts(total)
    normed[...] = (unit * small[5:6] + small[6:7]).astype(BF16)


def feed_kernel(near, far, g_near, g_far, w_up, bias, w_down, kept, sent, *rest):
    turns = ((far, g_far, sent, *rest[2:]), (near, g_near, kept, *rest[:2]))
    for rows, grad, out, acted, d_up in turns:
        up = mm(rows[...], w_up[...]) + bias[...]
        square = up * up
        bend = jnp.tanh(0.7978845608028654 * (up + 0.044715 * (up * square)))
        acted[...] = (0.5 * up * (1.0 + bend)).astype(BF16)
        slope = 0.5 * (1.0 + bend) + 0.5 * up * (1.0 - bend * bend) * (
            0.7978845608028654 * (1.0 + 0.134145 * square)
        )
        d_up[...] = (mm_t(grad[...], w_down[...]) * slope).astype(BF16)
        out[...] = mm_t(d_up[...], w_up[...]).astype(out.dtype)


def block_kernel(near, far, w_down, kept, sent):
    sent[...] = mm(far[...], w_down[...]).astype(BF16)
    kept[...] = mm(near[...], w_down[...])


def norm_two_kernel(kept, got, hidden, grad, small, d_hidden, d_attn, sums):
    incoming = kept[...] + got[...].astype(F32)
    unit, scale = norm_parts(hidden[...])
    total = grad[...].astype(F32) + norm_back(incoming, unit, scale, small[5:6])
    d_hidden[...] = total
    rounded = total.astype(BF16)
    d_attn[...] = rounded
    sums[...] = jnp.zeros(sums.shape, F32)
    sums[0:1] = jnp.sum(incoming * unit, axis=0, keepdims=True)
    sums[1:2] = jnp.sum(incoming, axis=0, keepdims=True)
    sums[2:3] = jnp.sum(rounded.astype(F32), axis=0, keepdims=True)
    sums[3:4] = jnp.sum(grad[...].astype(F32), axis=0, keepdims=True)


def outer_kernel(count, with_sums, *refs):
    out = refs[2 * count]
    out[...] = outer([r[...] for r in refs[:count]], [r[...] for r in refs[count : 2 * count]]).astype(BF16)
    if with_sums:
        total = 0.0
        for r in refs[count : 2 * count]:
            total = total + jnp.sum(r[...].astype(F32), axis=0, keepdims=True)
        refs[2 * count + 1][...] = total


def outer_call(lefts, rights, with_sums=False):
    dims = (lefts[0].shape[1], rights[0].shape[1])
    outs = [shape(dims, BF16)] + [shape((1, dims[1]), F32)] * with_sums
    flops = 2 * sum(v.shape[0] for v in lefts) * dims[0] * dims[1]
    kernel = functools.partial(outer_kernel, len(lefts), with_sums)
    return run(kernel, outs, list(lefts) + list(rights), flops)


def attend_back_kernel(fs_size, *refs):
    chunks, x_chunks, refs = refs[:fs_size], refs[fs_size : 2 * fs_size], refs[2 * fs_size :]
    query, key, value, probs, w_qk, w_v, w_out, kept, *sent = refs[: 7 + fs_size]
    d_qk, d_value, d_attn, sums, head_sums, d_context = refs[7 + fs_size :]
    step = kept.shape[0]
    rows, cols = query.shape
    for s, chunk in enumerate(chunks):
        d_attn[s * step : (s + 1) * step] = chunk[...]
    d_context[...] = mm_t(d_attn[...], w_out[...]).astype(BF16)
    for h in range(cols // HD):
        part = slice(h * HD, (h + 1) * HD)
        low = slice(cols + h * HD, cols + (h + 1) * HD)
        p = probs[h]
        d_value[:, part] = outer([p.astype(BF16)], [d_context[:, part]]).astype(BF16)
        d_probs = mm_t(d_context[:, part], value[:, part])
        d_score = p * (d_probs - jnp.sum(p * d_probs, axis=-1, keepdims=True))
        d_score = d_score.astype(BF16)
        d_qk[:, part] = (mm(d_score, key[:, part]) * HD**-0.5).astype(BF16)
        d_qk[:, low] = (outer([d_score], [query[:, part]]) * HD**-0.5).astype(BF16)
    head_sums[...] = jnp.zeros(head_sums.shape, F32)
    head_sums[0:1] = jnp.sum(d_qk[:, :cols].astype(F32), axis=0, keepdims=True)
    head_sums[1:2] = jnp.sum(d_value[...].astype(F32), axis=0, keepdims=True)
    sums[...] = jnp.zeros(sums.shape, F32)
    for s, out in enumerate([kept, *sent]):
        at = slice(s * step, (s + 1) * step)
        d_normed = mm_t(d_qk[at], w_qk[...]) + mm_t(d_value[at], w_v[...])
        out[...] = d_normed.astype(out.dtype)
        unit, _ = norm_parts(x_chunks[s][...].astype(F32))
        sums[0:1] += jnp.sum(d_normed * unit, axis=0, keepdims=True)
        sums[1:2] += jnp.sum(d_normed, axis=0, keepdims=True)


def norm_one_kernel(fs_size, x, d_hidden, kept, *refs):
    got, (small, out) = refs[: fs_size - 1], refs[fs_size - 1 :]
    incoming = kept[...]
    for piece in got:
        incoming = incoming + piece[...].astype(F32)
    unit, scale = norm_parts(x[...].astype(F32))
    out[...] = (d_hidden[...] + norm_back(incoming, unit, scale, small[0:1])).astype(BF16)


def pack(vectors, own):
    lead = vectors[0].shape[:-1]
    if own >= len(vectors):
        spare = [LANES - v.shape[-1] for v in vectors]
        rows = [jnp.pad(v, [(0, 0)] * len(lead) + [(0, n)]) for v, n in zip(vectors, spare)]
        block = jnp.stack(rows, axis=-2)
        return jnp.pad(block, [(0, 0)] * len(lead) + [(0, own - len(vectors)), (0, 0)])
    block = jnp.concatenate(vectors, axis=-1)
    block = jnp.pad(block, [(0, 0)] * len(lead) + [(0, own * LANES - block.shape[-1])])
    return block.reshape(lead + (own, LANES))


def unpack(block, own, own_ff):
    lead = block.shape[:-2]
    if own >= 9:
        return block[..., :8, :own], block[..., 8, :own_ff]
    block = block.reshape(lead + (-1,))
    return block[..., : 8 * own].reshape(lead + (8, own)), block[..., 8 * own : 8 * own + own_ff]


def heads_of(rows):
    return rows.reshape(rows.shape[0], -1, HD).transpose(1, 0, 2)


def rows_of(heads):
    return heads.transpose(1, 0, 2).reshape(heads.shape[1], -1)


def body(
    tokens,
    lengths,
    ln1_gain,
    ln1_shift,
    w_qkv,
    q_bias,
    v_bias,
    w_out,
    out_bias,
    ln2_gain,
    ln2_shift,
    w_up,
    up_bias,
    w_down,
    down_bias,
    cotangent,
):
    micro_count, tok_rows, width = tokens.shape
    dp_size, fs_size = lax.axis_size("dp"), lax.axis_size("fsdp")
    dp_at, fs_at = lax.axis_index("dp"), lax.axis_index("fsdp")
    own = w_qkv.shape[0]
    own_ff = w_down.shape[0]
    hidden_dev = w_up.shape[1] // dp_size
    head_cols = width // fs_size
    micros = range(micro_count)
    orders = bit_orders(dp_size)

    vectors = [ln1_gain, ln1_shift, q_bias, v_bias, out_bias, ln2_gain, ln2_shift, down_bias, up_bias]
    here = fs_at[None].astype(jnp.int32)
    toks = [tokens[m] for m in micros]
    cots = [cotangent[m] for m in micros]
    cut = 2 * head_cols
    block = shape((own, 3 * head_cols + LANES), BF16)
    sent = run(
        functools.partial(split_kernel, fs_size),
        [block] * fs_size,
        [here, w_qkv, pack(vectors, own)],
        w_qkv.size,
        smem=1,
    )
    sent, w_up = together(sent, w_up)
    got = list(sent[:1]) + [
        lax.ppermute(piece, "fsdp", shift_perm(fs_size, s)) for s, piece in enumerate(sent[1:], 1)
    ]
    up_rows = lax.all_to_all(w_up.reshape(own, dp_size, hidden_dev).transpose(1, 0, 2), "dp", 0, 0)
    swap = [(i, (i % dp_size) * fs_size + i // dp_size) for i in range(dp_size * fs_size)]
    out_part = lax.ppermute(w_out, BOTH, swap)
    got, out_part, toks = together(got, out_part, toks)
    out_part = out_part.reshape(own, fs_size, head_cols).transpose(1, 0, 2).reshape(-1, head_cols)
    x_all = [ring_gather(toks[m]) for m in micros]
    split = jnp.stack(got[::-1] + got[::-1])
    split = lax.dynamic_slice_in_dim(split, fs_size - 1 - fs_at, fs_size).reshape(fs_size * own, -1)
    first = dp_gather(split[:, : cut + LANES], orders[0])
    second = dp_gather(jnp.concatenate([split[:, cut + LANES :], out_part], axis=1), orders[1])
    x_all[-1], up_rows = together(x_all[-1], up_rows)
    up_here = lax.all_gather(up_rows, "fsdp", axis=0)
    up_here = up_here.transpose(1, 0, 2, 3).reshape(width, hidden_dev)
    qk_here = first[:, :cut]
    v_here = second[:, :head_cols]
    out_here = second[:, head_cols:].reshape(dp_size, fs_size, own, head_cols)
    out_here = out_here.transpose(0, 2, 1, 3).reshape(head_cols, width)
    small, bias_up = unpack(
        first[:, cut:].reshape(dp_size * fs_size, own, LANES).astype(F32), own, own_ff
    )
    small = small.transpose(1, 0, 2).reshape(8, width)
    biases = lax.dynamic_slice(small, (2, fs_at * head_cols), (2, head_cols))
    bias_up = lax.dynamic_slice_in_dim(bias_up.reshape(1, -1), dp_at * hidden_dev, hidden_dev, 1)

    bound = jnp.cumsum(lengths[:, 0], axis=1)
    head_ids = fs_at * (H // fs_size) + jnp.arange(H // fs_size)
    slopes = jnp.exp2(-8.0 * (head_ids.astype(F32) + 1.0) / H)
    rows = fs_size * tok_rows
    own_rows = shape((tok_rows, width), F32)
    low_rows = shape((tok_rows, width), BF16)
    pieces = [own_rows] + [low_rows] * (fs_size - 1)
    head_rows = shape((rows, head_cols), BF16)
    saved, hiddens, normed_twos = [], [], []
    for m in micros:
        meta = jnp.concatenate([here, bound[m]])
        outs = [shape((rows, width), BF16), head_rows, head_rows, head_rows]
        outs += [shape((H // fs_size, rows, rows), F32), head_rows]
        kept, *parts = run(
            functools.partial(attend_kernel, fs_size),
            pieces + outs,
            [meta, slopes] + x_all[m] + [small, biases, qk_here, v_here, out_here],
            8 * rows * width * head_cols + 4 * rows * rows * head_cols,
            smem=2,
        )
        sent, saving = parts[: fs_size - 1], parts[fs_size - 1 :]
        if m == 0:
            kept, cots = together(kept, cots)
        hidden, normed_two = run(
            functools.partial(hidden_kernel, fs_size),
            [own_rows, low_rows],
            [toks[m], kept] + ring_return(sent) + [small],
            20 * tok_rows * width,
        )
        saved.append(saving)
        hiddens.append(hidden)
        normed_twos.append(normed_two)

    hiddens[0], w_down = together(hiddens[0], w_down)
    g_all = [cube_gather(cots[m], orders[m % 2]) for m in micros]
    down_here = lax.all_gather(w_down, "fsdp", axis=0, tiled=True)
    half = dp_size // 2 * tok_rows
    halves = [shape((half, width), F32), shape((half, width), BF16)]
    normed_all = [cube_gather(normed_twos[m], orders[m % 2]) for m in micros]
    fed, d_hiddens, d_attns, sums_two = [], [], [], []
    for m in micros:
        kept, sent, *rest = run(
            feed_kernel,
            halves + [shape((half, hidden_dev), BF16)] * 4,
            [*normed_all[m], *g_all[m], up_here, bias_up, down_here],
            12 * half * width * hidden_dev,
        )
        fed.append(rest)
        kept, got = cube_scatter(kept, sent, orders[m % 2])
        d_hidden, d_attn, sums = run(
            norm_two_kernel,
            [own_rows, low_rows, shape((8, width), F32)],
            [kept, got, hiddens[m], cots[m], small],
            30 * tok_rows * width,
        )
        d_hiddens.append(d_hidden)
        d_attns.append(d_attn)
        sums_two.append(sums)
    acted = [(part[0], part[2]) for part in fed]
    d_ups = [(part[1], part[3]) for part in fed]
    flat = lambda pairs: [item for pair in pairs for item in pair]
    (grad_down,) = outer_call(flat(acted), flat(g_all))
    grad_down = lax.psum_scatter(grad_down, "fsdp", scatter_dimension=0, tiled=True)
    d_attns, acted, d_ups = together(d_attns, acted, d_ups)
    d_attn_all = [ring_gather(d_attns[m]) for m in micros]
    blocks = []
    for m in micros:
        kept, sent = run(block_kernel, halves, [*acted[m], down_here], 4 * half * width * hidden_dev)
        blocks.append(cube_scatter(kept, sent, orders[m % 2]))
    grad_up, d_up_bias = outer_call(flat(normed_all), flat(d_ups), True)
    grad_up = grad_up.reshape(dp_size, fs_size, own, hidden_dev).transpose(1, 0, 2, 3)
    grad_up = grad_up.reshape(width, hidden_dev)
    d_attn_all, grad_up, blocks = together(d_attn_all, grad_up, blocks)
    grad_up = lax.psum_scatter(grad_up, "fsdp", scatter_dimension=0, tiled=True)
    outputs = [
        (hiddens[m] + blocks[m][0] + blocks[m][1].astype(F32) + small[7:8]).astype(BF16) for m in micros
    ]

    grad_rows, backs = [], []
    for m in micros:
        normed, query, key, value, probs, context = saved[m]
        outs = [shape((rows, 2 * head_cols), BF16), head_rows, shape((rows, width), BF16)]
        outs += [shape((8, width), F32), shape((8, head_cols), F32)]
        kept, *parts = run(
            functools.partial(attend_back_kernel, fs_size),
            pieces + outs,
            d_attn_all[m]
            + x_all[m]
            + [query, key, value, probs, qk_here, v_here, out_here],
            8 * rows * width * head_cols + 8 * rows * rows * head_cols,
            scratch=[pltpu.VMEM((rows, head_cols), BF16)],
        )
        sent, back = parts[: fs_size - 1], parts[fs_size - 1 :]
        backs.append(back)
        (grad_row,) = run(
            functools.partial(norm_one_kernel, fs_size),
            [low_rows],
            [toks[m], d_hiddens[m], kept] + ring_return(sent) + [small],
            30 * tok_rows * width,
        )
        grad_rows.append(grad_row)
    d_qk_all, d_value_all, d_attn_rows, sums_one, head_sums = zip(*backs)
    grad_up = lax.all_to_all(grad_up.reshape(dp_size, own, hidden_dev), "dp", 0, 0)
    grad_up = grad_up.transpose(1, 0, 2).reshape(own, -1).astype(F32)

    d_gain_two, d_shift_two, d_out_bias, d_down_bias = sum(sums_two[1:], sums_two[0])[:4]
    d_gain_one, d_shift_one = sum(sums_one[1:], sums_one[0])[:2]
    d_q_bias, d_v_bias = sum(head_sums[1:], head_sums[0])[:2]

    def spread(part, total, at):
        return lax.dynamic_update_slice_in_dim(jnp.zeros((total,), F32), part, at, 0)

    d_q_bias = spread(d_q_bias, width, fs_at * head_cols)
    d_v_bias = spread(d_v_bias, width, fs_at * head_cols)
    d_up_bias = spread(d_up_bias[0], dp_size * hidden_dev, dp_at * hidden_dev)
    terms = [d_gain_one, d_shift_one, d_q_bias, d_v_bias]
    terms += [d_out_bias, d_gain_two, d_shift_two, d_down_bias, d_up_bias]
    terms = pack([t.reshape(dp_size * fs_size, -1) for t in terms], own).reshape(width, LANES)
    normed_all = [part[0] for part in saved]
    (grad_out,) = outer_call([part[5] for part in saved], d_attn_rows)
    grad_out = grad_out.reshape(dp_size, own, fs_size, head_cols).transpose(0, 2, 1, 3)
    (second,) = outer_call(normed_all, d_value_all)
    second = jnp.concatenate([second, grad_out.reshape(width, head_cols)], axis=1)
    second = dp_scatter(second, orders[1]).astype(BF16)
    grad_out = second[:, head_cols:].reshape(fs_size, own, head_cols).transpose(1, 0, 2)
    grad_out = lax.ppermute(grad_out.reshape(own, width), BOTH, [(b, a) for a, b in swap])
    grad_out = grad_out.astype(F32)
    (first,) = outer_call(normed_all, d_qk_all)
    first = dp_scatter(jnp.concatenate([first, terms.astype(BF16)], axis=1), orders[0]).astype(BF16)
    split = jnp.concatenate([first, second[:, :head_cols]], axis=1).reshape(fs_size, own, -1)
    sent = [lax.dynamic_index_in_dim(split, (fs_at + s) % fs_size, 0, False) for s in range(fs_size)]
    got = list(sent[:1]) + [
        lax.ppermute(piece, "fsdp", shift_perm(fs_size, s)) for s, piece in enumerate(sent[1:], 1)
    ]
    grad_qkv, terms = run(
        functools.partial(join_kernel, fs_size),
        [shape((own, 3 * width), F32), shape((own, LANES), F32)],
        [here] + got,
        own * 3 * width,
        smem=1,
    )
    terms, d_up_bias = unpack(terms, own, own_ff)
    d_gain_one, d_shift_one, d_q_bias, d_v_bias, d_out_bias, d_gain_two, d_shift_two, d_down_bias = terms
    return (
        jnp.stack(outputs, axis=0),
        jnp.stack(grad_rows, axis=0),
        d_gain_one,
        d_shift_one,
        grad_qkv,
        d_q_bias,
        d_v_bias,
        grad_out,
        d_out_bias,
        d_gain_two,
        d_shift_two,
        grad_up,
        d_up_bias,
        grad_down.astype(F32),
        d_down_bias,
    )


def solution(mesh):
    both = P(BOTH)
    rows = P(BOTH, None)
    toks = P(None, BOTH, None)
    return jax.shard_map(
        body,
        mesh=mesh,
        in_specs=(
            toks,
            P(None, "dp", None),
            both,
            both,
            rows,
            both,
            both,
            rows,
            both,
            both,
            both,
            rows,
            both,
            rows,
            both,
            toks,
        ),
        out_specs=(
            toks,
            toks,
            both,
            both,
            rows,
            both,
            both,
            rows,
            both,
            both,
            both,
            rows,
            both,
            rows,
            both,
        ),
        check_vma=False,
    )
```

```python
import functools

import jax
import jax.numpy as jnp
from jax import lax
from jax.experimental import pallas as pl
from jax.experimental.pallas import tpu as pltpu
from jax.sharding import PartitionSpec as P

H = 16
HD = 64
LANES = 128
F32 = jnp.float32
BIG = ("attend_kernel", "attend_back_kernel", "outer_kernel", "out_kernel")
BF16 = jnp.bfloat16
BOTH = ("dp", "fsdp")


def mm(left, right):
    return jnp.dot(left, right, preferred_element_type=F32)


def mm_t(left, right):
    return lax.dot_general(left, right, (((1,), (1,)), ((), ())), preferred_element_type=F32)


def outer(lefts, rights):
    total = None
    for left, right in zip(lefts, rights):
        part = lax.dot_general(left, right, (((0,), (0,)), ((), ())), preferred_element_type=F32)
        total = part if total is None else total + part
    return total


def norm_parts(values):
    centred = values - jnp.mean(values, axis=-1, keepdims=True)
    scale = lax.rsqrt(jnp.mean(centred * centred, axis=-1, keepdims=True) + 1e-05)
    return centred * scale, scale


def norm_back(grad, unit, scale, gain):
    inner = grad * gain
    return scale * (
        inner
        - jnp.mean(inner, axis=-1, keepdims=True)
        - unit * jnp.mean(inner * unit, axis=-1, keepdims=True)
    )


def shift_perm(size, step):
    return [(i, (i + step) % size) for i in range(size)]


def xor_perm(size, bit):
    return [(i, i ^ bit) for i in range(size)]


def ring_gather(rows):
    size = lax.axis_size("fsdp")
    return [rows] + [lax.ppermute(rows, "fsdp", shift_perm(size, s)) for s in range(1, size)]


def ring_return(sent):
    size = lax.axis_size("fsdp")
    return [lax.ppermute(p, "fsdp", shift_perm(size, size - s)) for s, p in enumerate(sent, 1)]


def bit_orders(size):
    bits = [1 << k for k in range(size.bit_length() - 1)]
    far, near = bits[1:], bits[:1]
    return [far + near, far[::-1] + near]


def cube_gather(rows, bits):
    size = lax.axis_size("dp")
    for bit in bits[:-1]:
        rows = join_rows(rows, lax.ppermute(rows, "dp", xor_perm(size, bit)))
    return rows, lax.ppermute(rows, "dp", xor_perm(size, bits[-1]))


def cube_step(parts, orders, step):
    size = lax.axis_size("dp")
    turns = [orders[m % 2][-1 - step] for m in range(len(parts))]
    got = [lax.ppermute(sent, "dp", xor_perm(size, bit)) for (_, sent), bit in zip(parts, turns)]
    if turns[0] == orders[0][0]:
        return [(kept, piece) for (kept, _), piece in zip(parts, got)]
    return [add_split(kept, piece) for (kept, _), piece in zip(parts, got)]


def dp_gather(block, bits):
    size = lax.axis_size("dp")
    place = lax.axis_index("dp")
    done = []
    for bit in bits:
        other = lax.ppermute(block, "dp", xor_perm(size, bit))
        high = (place & bit) != 0
        axis = sum(b > bit for b in done)
        block = jnp.stack([jnp.where(high, other, block), jnp.where(high, block, other)], axis=axis)
        done.append(bit)
    return block.reshape(-1, block.shape[-1])


def dp_scatter(part, bits):
    size = lax.axis_size("dp")
    place = lax.axis_index("dp")
    left = sorted(bits, reverse=True)
    part = part.reshape((2,) * len(bits) + (part.shape[0] // size, part.shape[1]))
    for bit in bits[::-1]:
        axis = left.index(bit)
        left.remove(bit)
        mine = jnp.where((place & bit) != 0, 1, 0)
        sent = lax.dynamic_index_in_dim(part, 1 - mine, axis=axis, keepdims=False)
        kept = lax.dynamic_index_in_dim(part, mine, axis=axis, keepdims=False)
        got = lax.ppermute(sent.astype(BF16), "dp", xor_perm(size, bit))
        part = kept.astype(F32) + got.astype(F32)
    return part


def pack(vectors, own):
    lead = vectors[0].shape[:-1]
    if own >= len(vectors):
        spare = [LANES - v.shape[-1] for v in vectors]
        rows = [jnp.pad(v, [(0, 0)] * len(lead) + [(0, n)]) for v, n in zip(vectors, spare)]
        block = jnp.stack(rows, axis=-2)
        return jnp.pad(block, [(0, 0)] * len(lead) + [(0, own - len(vectors)), (0, 0)])
    block = jnp.concatenate(vectors, axis=-1)
    block = jnp.pad(block, [(0, 0)] * len(lead) + [(0, own * LANES - block.shape[-1])])
    return block.reshape(lead + (own, LANES))


def unpack(block, own, own_ff):
    lead = block.shape[:-2]
    if own >= 9:
        return block[..., :8, :own], block[..., 8, :own_ff]
    block = block.reshape(lead + (-1,))
    return block[..., : 8 * own].reshape(lead + (8, own)), block[..., 8 * own : 8 * own + own_ff]


def run(kernel, outs, ins, flops, scratch=(), smem=0, after=()):
    name = getattr(kernel, "func", kernel).__name__
    big = name in BIG
    moved = sum(v.size * v.dtype.itemsize for v in list(outs) + list(ins))
    count = len(ins)

    def whole(dims):
        if big:
            return pl.BlockSpec(dims, lambda i: (0,) * len(dims))
        return pl.BlockSpec(memory_space=pltpu.VMEM)

    def body_kernel(*refs):
        kernel(*refs[:count], *refs[count + len(after) :])

    return pl.pallas_call(
        body_kernel,
        name=name,
        grid=(1,) * big,
        out_shape=outs,
        in_specs=[pl.BlockSpec(memory_space=pltpu.SMEM)] * smem
        + [whole(v.shape) for v in ins[smem:]]
        + [pl.BlockSpec(memory_space=pl.ANY)] * len(after),
        out_specs=[whole(v.shape) for v in outs],
        scratch_shapes=scratch,
        compiler_params=pltpu.CompilerParams(
            vmem_limit_bytes=60 * 1024 * 1024 if big else moved + 12 * 1024 * 1024
        ),
        cost_estimate=pl.CostEstimate(flops=int(flops), bytes_accessed=moved, transcendentals=0),
    )(*ins, *after)


def copy_kernel(*refs):
    for source, out in zip(refs, refs[len(refs) // 2 :]):
        out[...] = source[...]


def held(values, after):
    return run(copy_kernel, [shape(v.shape, v.dtype) for v in values], values, values[0].size, after=after)


def shape(dims, dtype):
    return jax.ShapeDtypeStruct(dims, dtype)


def add_split_kernel(kept, got, new_kept, new_sent):
    half = new_kept.shape[0]
    new_kept[...] = kept[:half] + got[:half].astype(F32)
    new_sent[...] = (kept[half:] + got[half:].astype(F32)).astype(BF16)


def join_kernel_rows(upper, lower, out):
    half = upper.shape[0]
    out[:half] = upper[...]
    out[half:] = lower[...]


def join_rows(upper, lower):
    out = shape((2 * upper.shape[0], upper.shape[1]), upper.dtype)
    return run(join_kernel_rows, [out], [upper, lower], upper.size)[0]


def add_split(kept, got):
    half = (kept.shape[0] // 2, kept.shape[1])
    return run(add_split_kernel, [shape(half, F32), shape(half, BF16)], [kept, got], kept.size)


def split_kernel(fs_size, at, w_qkv, small, *outs):
    cols = w_qkv.shape[1] // (3 * fs_size)
    for s, out in enumerate(outs):
        to = lax.rem(at[0] + s, fs_size) * cols
        for k, put in ((0, 0), (1, cols), (2, 2 * cols + LANES)):
            start = pl.multiple_of(to + k * fs_size * cols, LANES)
            out[:, put : put + cols] = w_qkv[:, pl.ds(start, cols)]
        out[:, 2 * cols : 2 * cols + LANES] = small[...]


def join_kernel(fs_size, at, *refs):
    pieces, (out, small) = refs[:fs_size], refs[fs_size:]
    cols = out.shape[1] // (3 * fs_size)
    total = 0.0
    for s, piece in enumerate(pieces):
        to = lax.rem(at[0] + fs_size - s, fs_size) * cols
        for k, put in ((0, 0), (1, cols), (2, 2 * cols + LANES)):
            start = pl.multiple_of(to + k * fs_size * cols, LANES)
            out[:, pl.ds(start, cols)] = piece[:, put : put + cols].astype(F32)
        total = total + piece[:, 2 * cols : 2 * cols + LANES].astype(F32)
    small[...] = total


def positions(meta, index, step, fs_size):
    place = index + meta[0] * step
    for s in range(1, fs_size):
        turn = jnp.where(meta[0] - s == -1, fs_size - 2, -2)
        place = place + jnp.where(index >= s * step, turn * step, 0)
    seg = jnp.zeros_like(index)
    for k in range(1, meta.shape[0]):
        seg = seg + jnp.where(place >= meta[k], 1, 0)
    return place, seg


def attend_kernel(fs_size, meta, slopes, *refs):
    chunks, refs = refs[:fs_size], refs[fs_size:]
    small, biases, first, second, w_out, kept, *sent = refs[: 5 + fs_size]
    unit, normed, mixed, probs, context = refs[5 + fs_size :]
    step = kept.shape[0]
    rows, cols = context.shape
    for s, chunk in enumerate(chunks):
        at = slice(s * step, (s + 1) * step)
        part, _ = norm_parts(chunk[...].astype(F32))
        unit[at] = part.astype(BF16)
        normed[at] = (part * small[0:1] + small[1:2]).astype(BF16)
    mixed[:, :cols] = (mm(normed[...], first[:, :cols]) + biases[0:1]).astype(BF16)
    mixed[:, cols : 2 * cols] = mm(normed[...], first[:, cols : 2 * cols]).astype(BF16)
    mixed[:, 2 * cols :] = (mm(normed[...], second[:, :cols]) + biases[1:2]).astype(BF16)
    row_place, row_seg = positions(meta, lax.broadcasted_iota(jnp.int32, (rows, 1), 0), step, fs_size)
    col_place, col_seg = positions(meta, lax.broadcasted_iota(jnp.int32, (1, rows), 1), step, fs_size)
    allowed = (row_seg == col_seg) & (col_place <= row_place)
    distance = (row_place - col_place).astype(F32)
    for h in range(cols // HD):
        query, key, value = [slice(k * cols + h * HD, k * cols + (h + 1) * HD) for k in range(3)]
        scores = mm_t(mixed[:, query], mixed[:, key]) * HD**-0.5 - slopes[h] * distance
        scores = jnp.where(allowed, scores, -1e30)
        scores = jnp.exp(scores - jnp.max(scores, axis=-1, keepdims=True))
        scores = scores / jnp.sum(scores, axis=-1, keepdims=True)
        probs[h] = scores
        context[:, query] = mm(scores.astype(BF16), mixed[:, value]).astype(BF16)
    kept[...] = mm(context[:step], w_out[...])
    for s, piece in enumerate(sent, 1):
        piece[...] = mm(context[s * step : (s + 1) * step], w_out[...]).astype(BF16)


def hidden_kernel(fs_size, x, kept, *refs):
    got, (small, hidden, normed) = refs[: fs_size - 1], refs[fs_size - 1 :]
    total = kept[...]
    for piece in got:
        total = total + piece[...].astype(F32)
    total = x[...].astype(F32) + total + small[4:5]
    hidden[...] = total
    unit, _ = norm_parts(total)
    normed[...] = (unit * small[5:6] + small[6:7]).astype(BF16)


def feed_kernel(near, far, g_near, g_far, w_up, bias, w_down, kept, sent, *rest):
    turns = ((far, g_far, sent, *rest[2:]), (near, g_near, kept, *rest[:2]))
    for rows, grad, out, acted, d_up in turns:
        up = mm(rows[...], w_up[...]) + bias[...]
        square = up * up
        bend = jnp.tanh(0.7978845608028654 * (up + 0.044715 * (up * square)))
        acted[...] = (0.5 * up * (1.0 + bend)).astype(BF16)
        slope = 0.5 * (1.0 + bend) + 0.5 * up * (1.0 - bend * bend) * (
            0.7978845608028654 * (1.0 + 0.134145 * square)
        )
        d_up[...] = (mm_t(grad[...], w_down[...]) * slope).astype(BF16)
        out[...] = mm_t(d_up[...], w_up[...]).astype(out.dtype)


def block_kernel(near, far, w_down, kept, sent):
    sent[...] = mm(far[...], w_down[...]).astype(BF16)
    kept[...] = mm(near[...], w_down[...])


def norm_two_kernel(kept, got, hidden, grad, small, d_hidden, d_attn, sums):
    incoming = kept[...] + got[...].astype(F32)
    unit, scale = norm_parts(hidden[...])
    total = grad[...].astype(F32) + norm_back(incoming, unit, scale, small[5:6])
    d_hidden[...] = total
    rounded = total.astype(BF16)
    d_attn[...] = rounded
    sums[...] = jnp.zeros(sums.shape, F32)
    sums[0:1] = jnp.sum(incoming * unit, axis=0, keepdims=True)
    sums[1:2] = jnp.sum(incoming, axis=0, keepdims=True)
    sums[2:3] = jnp.sum(rounded.astype(F32), axis=0, keepdims=True)
    sums[3:4] = jnp.sum(grad[...].astype(F32), axis=0, keepdims=True)


def outer_kernel(count, with_sums, beside, *refs):
    lefts, rights, refs = refs[:count], refs[count : 2 * count], refs[2 * count :]
    out = refs[beside]
    cols = rights[0].shape[1]
    total = outer([r[...] for r in lefts], [r[...] for r in rights])
    out[:, :cols] = total.astype(BF16)
    if beside:
        out[:, cols:] = refs[0][...]
    if with_sums:
        total = 0.0
        for r in rights:
            total = total + jnp.sum(r[...].astype(F32), axis=0, keepdims=True)
        refs[beside + 1][...] = total


def outer_call(lefts, rights, with_sums=False, beside=(), after=()):
    dims = (lefts[0].shape[1], rights[0].shape[1])
    wide = dims[1] + sum(v.shape[1] for v in beside)
    outs = [shape((dims[0], wide), BF16)] + [shape((1, dims[1]), F32)] * with_sums
    flops = 2 * sum(v.shape[0] for v in lefts) * dims[0] * dims[1]
    kernel = functools.partial(outer_kernel, len(lefts), with_sums, len(beside))
    return run(kernel, outs, [*lefts, *rights, *beside], flops, after=after)


def out_kernel(fs_size, own, *refs):
    out, count = refs[-1], len(refs) // (fs_size + 1)
    total = 0.0
    for context, chunks in [(refs[k * (fs_size + 1)], refs[k * (fs_size + 1) + 1 :]) for k in range(count)]:
        step = chunks[0].shape[0]
        for s in range(fs_size):
            total = total + outer([context[s * step : (s + 1) * step]], [chunks[s][...]])
    if own % 16:
        out[...] = total.astype(BF16)
        return
    cols = out.shape[1]
    for k in range(total.shape[0] // own):
        for s in range(fs_size):
            part = total[k * own : (k + 1) * own, s * cols : (s + 1) * cols]
            at = (k * fs_size + s) * own
            out[at : at + own] = part.astype(BF16)


def attend_back_kernel(fs_size, *refs):
    chunks, refs = refs[:fs_size], refs[fs_size:]
    unit, mixed, probs, first, second, w_out, kept, *sent = refs[: 6 + fs_size]
    d_qk, d_value, sums, head_sums, d_context = refs[6 + fs_size :]
    step = kept.shape[0]
    cols = d_value.shape[1]
    for s, chunk in enumerate(chunks):
        d_context[s * step : (s + 1) * step] = mm_t(chunk[...], w_out[...]).astype(BF16)
    for h in range(cols // HD):
        query, key, value = [slice(k * cols + h * HD, k * cols + (h + 1) * HD) for k in range(3)]
        p = probs[h]
        d_value[:, query] = outer([p.astype(BF16)], [d_context[:, query]]).astype(BF16)
        d_probs = mm_t(d_context[:, query], mixed[:, value])
        d_score = p * (d_probs - jnp.sum(p * d_probs, axis=-1, keepdims=True))
        d_score = d_score.astype(BF16)
        d_qk[:, query] = (mm(d_score, mixed[:, key]) * HD**-0.5).astype(BF16)
        d_qk[:, key] = (outer([d_score], [mixed[:, query]]) * HD**-0.5).astype(BF16)
    head_sums[...] = jnp.zeros(head_sums.shape, F32)
    head_sums[0:1] = jnp.sum(d_qk[:, :cols].astype(F32), axis=0, keepdims=True)
    head_sums[1:2] = jnp.sum(d_value[...].astype(F32), axis=0, keepdims=True)
    sums[...] = jnp.zeros(sums.shape, F32)
    for s, out in enumerate([kept, *sent]):
        at = slice(s * step, (s + 1) * step)
        d_normed = mm_t(d_qk[at], first[:, : 2 * cols]) + mm_t(d_value[at], second[:, :cols])
        out[...] = d_normed.astype(out.dtype)
        sums[0:1] += jnp.sum(d_normed * unit[at].astype(F32), axis=0, keepdims=True)
        sums[1:2] += jnp.sum(d_normed, axis=0, keepdims=True)


def norm_one_kernel(fs_size, x, d_hidden, kept, *refs):
    got, (small, out) = refs[: fs_size - 1], refs[fs_size - 1 :]
    incoming = kept[...]
    for piece in got:
        incoming = incoming + piece[...].astype(F32)
    unit, scale = norm_parts(x[...].astype(F32))
    out[...] = (d_hidden[...] + norm_back(incoming, unit, scale, small[0:1])).astype(BF16)


def pack(vectors, own):
    lead = vectors[0].shape[:-1]
    if own >= len(vectors):
        spare = [LANES - v.shape[-1] for v in vectors]
        rows = [jnp.pad(v, [(0, 0)] * len(lead) + [(0, n)]) for v, n in zip(vectors, spare)]
        block = jnp.stack(rows, axis=-2)
        return jnp.pad(block, [(0, 0)] * len(lead) + [(0, own - len(vectors)), (0, 0)])
    block = jnp.concatenate(vectors, axis=-1)
    block = jnp.pad(block, [(0, 0)] * len(lead) + [(0, own * LANES - block.shape[-1])])
    return block.reshape(lead + (own, LANES))


def unpack(block, own, own_ff):
    lead = block.shape[:-2]
    if own >= 9:
        return block[..., :8, :own], block[..., 8, :own_ff]
    block = block.reshape(lead + (-1,))
    return block[..., : 8 * own].reshape(lead + (8, own)), block[..., 8 * own : 8 * own + own_ff]


def body(
    tokens,
    lengths,
    ln1_gain,
    ln1_shift,
    w_qkv,
    q_bias,
    v_bias,
    w_out,
    out_bias,
    ln2_gain,
    ln2_shift,
    w_up,
    up_bias,
    w_down,
    down_bias,
    cotangent,
):
    micro_count, tok_rows, width = tokens.shape
    dp_size, fs_size = lax.axis_size("dp"), lax.axis_size("fsdp")
    dp_at, fs_at = lax.axis_index("dp"), lax.axis_index("fsdp")
    own = w_qkv.shape[0]
    own_ff = w_down.shape[0]
    hidden_dev = w_up.shape[1] // dp_size
    head_cols = width // fs_size
    micros = range(micro_count)
    orders = bit_orders(dp_size)

    vectors = [ln1_gain, ln1_shift, q_bias, v_bias, out_bias, ln2_gain, ln2_shift, down_bias, up_bias]
    here = fs_at[None].astype(jnp.int32)
    toks = [tokens[m] for m in micros]
    cots = [cotangent[m] for m in micros]
    cut = 2 * head_cols
    block = shape((own, 3 * head_cols + LANES), BF16)
    sent = run(
        functools.partial(split_kernel, fs_size),
        [block] * fs_size,
        [here, w_qkv, pack(vectors, own)],
        w_qkv.size,
        smem=1,
    )
    down_here = lax.all_gather(w_down, "fsdp", axis=0, tiled=True)
    got = list(sent[:1]) + [
        lax.ppermute(piece, "fsdp", shift_perm(fs_size, s)) for s, piece in enumerate(sent[1:], 1)
    ]
    up_rows = lax.all_to_all(w_up.reshape(own, dp_size, hidden_dev).transpose(1, 0, 2), "dp", 0, 0)
    swap = [(i, (i % dp_size) * fs_size + i // dp_size) for i in range(dp_size * fs_size)]
    out_part = lax.ppermute(w_out, BOTH, swap)
    out_part = out_part.reshape(own, fs_size, head_cols).transpose(1, 0, 2).reshape(-1, head_cols)
    x_all = [ring_gather(toks[m]) for m in micros]
    split = jnp.stack(got[::-1] + got[::-1])
    split = lax.dynamic_slice_in_dim(split, fs_size - 1 - fs_at, fs_size).reshape(fs_size * own, -1)
    first = dp_gather(split[:, : cut + LANES], orders[0])
    second = dp_gather(jnp.concatenate([split[:, cut + LANES :], out_part], axis=1), orders[1])
    out_here = second[:, head_cols:].reshape(dp_size, fs_size, own, head_cols)
    out_here = out_here.transpose(0, 2, 1, 3).reshape(head_cols, width)
    small, bias_up = unpack(
        first[:, cut:].reshape(dp_size * fs_size, own, LANES).astype(F32), own, own_ff
    )
    small = small.transpose(1, 0, 2).reshape(8, width)
    biases = lax.dynamic_slice(small, (2, fs_at * head_cols), (2, head_cols))
    bias_up = lax.dynamic_slice_in_dim(bias_up.reshape(1, -1), dp_at * hidden_dev, hidden_dev, 1)

    bound = jnp.cumsum(lengths[:, 0], axis=1)
    head_ids = fs_at * (H // fs_size) + jnp.arange(H // fs_size)
    slopes = jnp.exp2(-8.0 * (head_ids.astype(F32) + 1.0) / H)
    rows = fs_size * tok_rows
    own_rows = shape((tok_rows, width), F32)
    low_rows = shape((tok_rows, width), BF16)
    pieces = [own_rows] + [low_rows] * (fs_size - 1)
    head_rows = shape((rows, head_cols), BF16)
    saved, hiddens, normed_twos, attended = [], [], [], []
    g_all = [cube_gather(cots[m], orders[m % 2]) for m in micros]
    flat = lambda groups: [item for group in groups for item in group]
    for m in micros:
        meta = jnp.concatenate([here, bound[m]])
        outs = [shape((rows, width), BF16)] * 2 + [shape((rows, 3 * head_cols), BF16)]
        outs += [shape((H // fs_size, rows, rows), F32), head_rows]
        kept, *parts = run(
            functools.partial(attend_kernel, fs_size),
            pieces + outs,
            [meta, slopes] + x_all[m] + [small, biases, first, second, out_here],
            8 * rows * width * head_cols + 4 * rows * rows * head_cols,
            smem=2,
            after=[attended[0][0]] if m else [],
        )
        attended.append((kept, parts[: fs_size - 1]))
        saved.append(parts[fs_size - 1 :])
    for m in micros:
        kept, sent = attended[m]
        hidden, normed_two = run(
            functools.partial(hidden_kernel, fs_size),
            [own_rows, low_rows],
            [toks[m], kept] + ring_return(sent) + [small],
            20 * tok_rows * width,
            after=[down_here] if m else [],
        )
        hiddens.append(hidden)
        normed_twos.append(normed_two)
    (up_rows,) = held([up_rows], hiddens[:1])
    up_here = lax.all_gather(up_rows, "fsdp", axis=0)
    up_here = up_here.transpose(1, 0, 2, 3).reshape(width, hidden_dev)

    half = dp_size // 2 * tok_rows
    halves = [shape((half, width), F32), shape((half, width), BF16)]
    normed_all = [cube_gather(normed_twos[m], orders[m % 2]) for m in micros]
    fed, parts, d_hiddens, d_attns, sums_two = [], [], [], [], []
    steps = dp_size.bit_length() - 1
    for m in micros:
        kept, sent, *rest = run(
            feed_kernel,
            halves + [shape((half, hidden_dev), BF16)] * 4,
            [*normed_all[m], *g_all[m], up_here, bias_up, down_here],
            12 * half * width * hidden_dev,
        )
        fed.append(rest)
        parts.append((kept, sent))
    acted = [(part[0], part[2]) for part in fed]
    d_ups = [(part[1], part[3]) for part in fed]
    for k in range(steps):
        parts = cube_step(parts, orders, k)
        if k == 0:
            (grad_down,) = outer_call(flat(acted), flat(g_all), after=flat(parts))
    grad_down_all = grad_down
    grad_down = lax.psum_scatter(grad_down, "fsdp", scatter_dimension=0, tiled=True)
    for m in micros:
        d_hidden, d_attn, sums = run(
            norm_two_kernel,
            [own_rows, low_rows, shape((8, width), F32)],
            [*parts[m], hiddens[m], cots[m], small],
            30 * tok_rows * width,
            after=[grad_down_all],
        )
        d_hiddens.append(d_hidden)
        d_attns.append(d_attn)
        sums_two.append(sums)
    d_attn_all = [ring_gather(d_attns[m]) for m in micros]
    grad_up, d_up_bias = outer_call(flat(normed_all), flat(d_ups), True, after=d_attns)
    grad_up = grad_up.reshape(dp_size, fs_size, own, hidden_dev).transpose(1, 0, 2, 3)
    grad_up = grad_up.reshape(width, hidden_dev)
    grad_up = lax.psum_scatter(grad_up, "fsdp", scatter_dimension=0, tiled=True)
    blocks = [
        run(
            block_kernel,
            halves,
            [*acted[m], down_here],
            4 * half * width * hidden_dev,
            after=d_attns,
        )
        for m in micros
    ]
    for k in range(steps):
        blocks = cube_step(blocks, orders, k)

    in_order = own % 16 == 0
    (grad_out,) = run(
        functools.partial(out_kernel, fs_size, own),
        [shape((width, head_cols) if in_order else (head_cols, width), BF16)],
        flat([[saved[m][4], *d_attn_all[m]] for m in micros]),
        2 * micro_count * rows * width * head_cols,
    )
    if not in_order:
        grad_out = grad_out.reshape(dp_size, own, fs_size, head_cols).transpose(0, 2, 1, 3)
        grad_out = grad_out.reshape(width, head_cols)
    returned, backs = [], []
    for m in micros:
        unit, _, mixed, probs, _ = saved[m]
        outs = [shape((rows, 2 * head_cols), BF16), head_rows]
        outs += [shape((8, width), F32), shape((8, head_cols), F32)]
        kept, *parts = run(
            functools.partial(attend_back_kernel, fs_size),
            pieces + outs,
            d_attn_all[m]
            + [unit, mixed, probs, first, second, out_here],
            8 * rows * width * head_cols + 8 * rows * rows * head_cols,
            scratch=[pltpu.VMEM((rows, head_cols), BF16)],
            after=[grad_out, *flat(blocks)] if m else flat(d_attn_all[1:]) + [grad_down],
        )
        backs.append(parts[fs_size - 1 :])
        returned.append((kept, ring_return(parts[: fs_size - 1])))
    d_qk_all, d_value_all, sums_one, head_sums = zip(*backs)
    outputs = [
        (hiddens[m] + blocks[m][0] + blocks[m][1].astype(F32) + small[7:8]).astype(BF16) for m in micros
    ]
    grad_up = lax.all_to_all(grad_up.reshape(dp_size, own, hidden_dev), "dp", 0, 0)

    d_gain_two, d_shift_two, d_out_bias, d_down_bias = sum(sums_two[1:], sums_two[0])[:4]
    d_gain_one, d_shift_one = sum(sums_one[1:], sums_one[0])[:2]
    d_q_bias, d_v_bias = sum(head_sums[1:], head_sums[0])[:2]

    def spread(part, total, at):
        return lax.dynamic_update_slice_in_dim(jnp.zeros((total,), F32), part, at, 0)

    d_q_bias = spread(d_q_bias, width, fs_at * head_cols)
    d_v_bias = spread(d_v_bias, width, fs_at * head_cols)
    d_up_bias = spread(d_up_bias[0], dp_size * hidden_dev, dp_at * hidden_dev)
    terms = [d_gain_one, d_shift_one, d_q_bias, d_v_bias]
    terms += [d_out_bias, d_gain_two, d_shift_two, d_down_bias, d_up_bias]
    terms = pack([t.reshape(dp_size * fs_size, -1) for t in terms], own).reshape(width, LANES)
    normed_all = [part[1] for part in saved]
    (second,) = outer_call(normed_all, d_value_all, beside=[grad_out])
    second = dp_scatter(second, orders[1]).astype(BF16)
    grad_out = second[:, head_cols:].reshape(fs_size, own, head_cols).transpose(1, 0, 2)
    grad_out = lax.ppermute(grad_out.reshape(own, width), BOTH, [(b, a) for a, b in swap])
    grad_out = grad_out.astype(F32)
    (first,) = outer_call(
        normed_all, d_qk_all, beside=[terms.astype(BF16)]
    )
    first = dp_scatter(first, orders[0]).astype(BF16)
    split = jnp.concatenate([first, second[:, :head_cols]], axis=1).reshape(fs_size, own, -1)
    sent = [lax.dynamic_index_in_dim(split, (fs_at + s) % fs_size, 0, False) for s in range(fs_size)]
    grad_rows = [
        run(
            functools.partial(norm_one_kernel, fs_size),
            [low_rows],
            [toks[m], d_hiddens[m], returned[m][0], *returned[m][1], small],
            30 * tok_rows * width,
            after=[split],
        )[0]
        for m in micros
    ]
    grad_up = grad_up.transpose(1, 0, 2).reshape(own, -1).astype(F32)
    got = list(sent[:1]) + [
        lax.ppermute(piece, "fsdp", shift_perm(fs_size, s)) for s, piece in enumerate(sent[1:], 1)
    ]
    grad_qkv, terms = run(
        functools.partial(join_kernel, fs_size),
        [shape((own, 3 * width), F32), shape((own, LANES), F32)],
        [here] + got,
        own * 3 * width,
        smem=1,
    )
    terms, d_up_bias = unpack(terms, own, own_ff)
    d_gain_one, d_shift_one, d_q_bias, d_v_bias, d_out_bias, d_gain_two, d_shift_two, d_down_bias = terms
    return (
        jnp.stack(outputs, axis=0),
        jnp.stack(grad_rows, axis=0),
        d_gain_one,
        d_shift_one,
        grad_qkv,
        d_q_bias,
        d_v_bias,
        grad_out,
        d_out_bias,
        d_gain_two,
        d_shift_two,
        grad_up,
        d_up_bias,
        grad_down.astype(F32),
        d_down_bias,
    )


def solution(mesh):
    both = P(BOTH)
    rows = P(BOTH, None)
    toks = P(None, BOTH, None)
    return jax.shard_map(
        body,
        mesh=mesh,
        in_specs=(
            toks,
            P(None, "dp", None),
            both,
            both,
            rows,
            both,
            both,
            rows,
            both,
            both,
            both,
            rows,
            both,
            rows,
            both,
            toks,
        ),
        out_specs=(
            toks,
            toks,
            both,
            both,
            rows,
            both,
            both,
            rows,
            both,
            both,
            both,
            rows,
            both,
            rows,
            both,
        ),
        check_vma=False,
    )
```
